32 devices in a mesh: freq: 4 (over x, core), tile: 8 (over z, y).
Axes of the slice: x: 2, y: 2, z: 4, core: 2. Of those that a mesh axis runs over, the one named last changes fastest.
Arguments:
- virtual_source_trace: bfloat16 [128, 4, 8400], P(('freq', 'tile')), may hold values from -6 to 6
- v_bases: bfloat16 [4, 192, 120, 2, 32, 70], P('freq', 'tile'), may hold values from -0.75 to 0.75
- u_bases: bfloat16 [4, 192, 120, 2, 32, 70], P('freq', 'tile'), may hold values from -0.09375 to 0.09375
- ranks: int32 [4, 192, 120], P('freq', 'tile'), may hold values from 16 to 32, as said below
- freq_bin: int32 [4], replicated, may hold values from 1 to 63
- slab_order: int32 [32], replicated, may hold values from 0 to 31, each once
Outputs:
- redatumed: bfloat16 [128, 4, 13440], P(('freq', 'tile'))
The draws below stay inside these ranges and needn't reach their ends.
Inputs may be any that keep to these rules, and one draw needn't show every extreme that they name: `ranks`: every rank is 16 or 32.
All inputs are finite; a program needn't handle non-finite values.
Results may differ from the reference program's by a relative error of at most 0.008.
Values may be sent and summed in bfloat16 or wider, within the bound.
No kernel may reach another device: no remote copies, remote signals or barrier semaphores. Data moves between devices by JAX's collectives and lax.ppermute only.
A program may use at most 192 MiB of HBM per device.

```python
import math
import jax
import jax.numpy as jnp
from jax import lax

TILE_EXTENT = 70
TILE_ROWS = 192
TILE_COLUMNS = 120
RBLOCK = 16
VIRTUAL_SOURCES = 4
TIME_DEV = 4
RMAX = 32
SOURCE_COUNT = 8400
WINDOW_FREQS = 4
TIME_SAMPLES = 128
DEVICES = 32


def draw_ranks(key, part):
    level_key = jax.random.fold_in(key, 11)
    tile_key = jax.random.fold_in(key, 23)
    levels = jax.random.randint(level_key, (WINDOW_FREQS, 1, 1), 0, 5)
    tickets = jax.random.randint(tile_key, (WINDOW_FREQS, TILE_ROWS, TILE_COLUMNS), 0, 4)
    return (RBLOCK + RBLOCK * (tickets < levels).astype(jnp.int32)).astype(jnp.int32)


def with_ends(entries, stream_key, smallest, largest):
    dims = entries.shape
    place = [jax.random.randint(jax.random.fold_in(stream_key, axis), (), 0, dims[axis]) for axis in range(len(dims))]
    entries = entries.at[tuple(place)].set(smallest)
    longest = dims.index(max(dims))
    place[longest] = (place[longest] + 1) % dims[longest]
    return entries.at[tuple(place)].set(largest)


def block_scale(rng, extent, pieces, smallest, top_value):
    def one(dim, shards_of):
        heights = jax.random.uniform(jax.random.fold_in(jax.random.fold_in(rng, 6), dim), (shards_of,), jnp.float32, smallest / len(pieces), top_value / len(pieces))
        return jnp.repeat(jnp.exp(heights), extent[dim] // shards_of).reshape((-1,) + (1,) * (len(extent) - dim - 1))

    factor_of = one(*pieces[0])
    for cut in pieces[1:]:
        factor_of = factor_of * one(*cut)
    return factor_of


def bell_draw(stream_key, extent, width, reach, cuts=(), kind=jnp.bfloat16):
    drawn = jax.random.normal(stream_key, extent, jnp.float32) * width
    if len(cuts) > 0:
        drawn = block_scale(stream_key, extent, cuts, -0.22, 0.18) * drawn
    return jnp.clip(drawn, min=-reach, max=reach).astype(kind)


def setup_inputs(seed: int = 0) -> dict:
    key_list = jax.random.split(jax.random.key(seed), 7)
    virtual_source_trace = bell_draw(key_list[0], (TIME_SAMPLES, VIRTUAL_SOURCES, SOURCE_COUNT), 1.0, 6.0, ((0, 32),))
    v_bases = bell_draw(key_list[1], (WINDOW_FREQS, TILE_ROWS, TILE_COLUMNS, 2, RMAX, TILE_EXTENT), TILE_EXTENT ** -0.5, 0.75, ((0, 4), (1, 8)))
    u_bases = bell_draw(key_list[2], (WINDOW_FREQS, TILE_ROWS, TILE_COLUMNS, 2, RMAX, TILE_EXTENT), (RMAX * TILE_COLUMNS) ** -0.5, 0.09375, ((0, 4), (1, 8)))
    ranks = draw_ranks(jax.random.fold_in(key_list[6], 71), 0)
    freq_bin = with_ends(jax.random.randint(key_list[4], (WINDOW_FREQS,), 1, TIME_SAMPLES // 2), jax.random.fold_in(key_list[4], 1), 1, (TIME_SAMPLES // 2) - 1).astype(jnp.int32)
    slab_order = jax.random.permutation(key_list[5], DEVICES).astype(jnp.int32)
    return dict(virtual_source_trace=virtual_source_trace, v_bases=v_bases, u_bases=u_bases, ranks=ranks, freq_bin=freq_bin, slab_order=slab_order)


def angles_of(freq_bin, times, total):
    products = freq_bin[:, None] * times[None, :] % total
    return products.astype(jnp.float32) * (2.0 * math.pi / total)

def rounded(values):
    return lax.optimization_barrier(values.astype(jnp.bfloat16)).astype(jnp.float32)

def apply_kernel(operands):
    v_part, u_part, rank_part, spec_part = operands
    basis_re = v_part[:, :, 0].astype(jnp.float32)
    basis_im = v_part[:, :, 1].astype(jnp.float32)
    left_re = u_part[:, :, 0].astype(jnp.float32)
    left_im = u_part[:, :, 1].astype(jnp.float32)
    spec_re = spec_part[0].astype(jnp.float32)
    spec_im = spec_part[1].astype(jnp.float32)

    def project(factor_basis, spec):
        return jnp.einsum('ijrp,vjp->ijrv', factor_basis, spec)
    coef_re = project(basis_re, spec_re) - project(basis_im, spec_im)
    coef_im = project(basis_re, spec_im) + project(basis_im, spec_re)
    rank_mask = (jnp.arange(RMAX, dtype=jnp.int32)[None, None, :] < rank_part[:, :, None]).astype(jnp.float32)[..., None]
    coef_re = rounded(coef_re * rank_mask)
    coef_im = rounded(coef_im * rank_mask)

    def expand(factor_basis, factor_weight):
        return jnp.einsum('debs,debm->mds', factor_basis, factor_weight).reshape(VIRTUAL_SOURCES, TILE_ROWS * TILE_EXTENT)
    out_re = expand(left_re, coef_re) - expand(left_im, coef_im)
    out_im = expand(left_re, coef_im) + expand(left_im, coef_re)
    return jnp.stack([out_re, out_im])

def reference(virtual_source_trace, v_bases, u_bases, ranks, freq_bin, slab_order):
    times = (slab_order[:, None] * TIME_DEV + jnp.arange(TIME_DEV, dtype=jnp.int32)[None, :]).reshape(TIME_SAMPLES).astype(jnp.int32)
    angles = angles_of(freq_bin.astype(jnp.int32), times, TIME_SAMPLES)
    forward = jnp.stack([jnp.cos(angles), -jnp.sin(angles)], axis=1) / math.sqrt(TIME_SAMPLES)
    frequency_spectra = jnp.einsum('fct,tvs->fcvs', forward, virtual_source_trace.astype(jnp.float32), precision=lax.Precision.HIGHEST)
    frequency_spectra = frequency_spectra.astype(jnp.bfloat16).reshape(WINDOW_FREQS, 2, VIRTUAL_SOURCES, TILE_COLUMNS, TILE_EXTENT)
    received = lax.map(apply_kernel, (v_bases, u_bases, ranks, frequency_spectra))
    inverse = jnp.stack([jnp.cos(angles.T), -jnp.sin(angles.T)], axis=2) / math.sqrt(WINDOW_FREQS)
    redatumed = jnp.einsum('tfc,fcvn->tvn', inverse, received, precision=lax.Precision.HIGHEST)
    return redatumed.astype(jnp.bfloat16)
```

```python
import functools
import math

import jax
import jax.numpy as jnp
from jax import lax
from jax.experimental import pallas as pl
from jax.experimental.pallas import tpu as pltpu
from jax.sharding import PartitionSpec as P

LANES = 128
PACK = 16
WAYS = 2


def round_up(value, step):
    return -(-value // step) * step


def step_of(count, most, multiple=1):
    return max(k for k in range(1, most + 1) if count % k == 0 and (k * multiple) % 8 == 0)


def fold(parts, piece, size):
    return jnp.concatenate([part[..., piece * size : (piece + 1) * size] for part in parts], axis=-1)


def right_kernel(shape, x_ref, rank_ref, v_ref, out_ref, xj, xp, xg, left, right, acc):
    sources, n_group, per_group, width, ways = shape
    count, _, block, ranks, columns = v_ref.shape
    step = pl.program_id(0)
    nv = 2 * sources
    size = LANES // ways
    parts = block // ways
    lane = lax.broadcasted_iota(jnp.int32, (size, LANES), 1) % size
    diagonal = lane == lax.broadcasted_iota(jnp.int32, (size, LANES), 0)

    @pl.when(step == 0)
    def _():
        xj[...] = jnp.zeros_like(xj)
        for g in range(n_group):
            for k in range(per_group):
                j = g * per_group + k
                if j < columns:
                    xj[j * nv : (j + 1) * nv, :width] = x_ref[g, :, k * width : (k + 1) * width]
        for v in range(nv):
            xp[v] = xj[pl.ds(v, LANES, nv), :].T
            rows = [xp[v, pl.ds(a, width // ways, ways), :] for a in range(ways)]
            for g in range(ways):
                xg[g, v] = fold(rows, g, size)

    blank = jnp.zeros((count * ranks, LANES - columns), jnp.bfloat16)
    for q in range(parts):
        for c in range(2):
            rows = [
                jnp.concatenate([v_ref[:, c, q * ways + a].reshape(count * ranks, columns), blank], axis=1)
                for a in range(ways)
            ]
            at = (q * 2 + c) * LANES
            for g in range(ways):
                left[g, :, at : at + LANES] = fold(rows, g, size)
                for v in range(nv):
                    take = v if c == 0 else (v + sources) % nv
                    row = xg[g, take, pl.ds(step * parts + q, 1), :]
                    if c == 1 and v < sources:
                        row = -row
                    right[g, v * size : (v + 1) * size, at : at + LANES] = jnp.where(
                        diagonal, row, 0.0
                    ).astype(jnp.bfloat16)
    for g in range(ways):
        product = lax.dot_general(
            left[g], right[g], (((1,), (1,)), ((), ())), preferred_element_type=jnp.float32
        )

        @pl.when(step == 0)
        def _():
            acc[g] = product

        @pl.when(step > 0)
        def _():
            acc[g] += product

    @pl.when(step == pl.num_programs(0) - 1)
    def _():
        @pl.loop(0, count)
        def _(i):
            rank = rank_ref[i]
            for h in range(ranks // PACK):
                first = pl.multiple_of(i * ranks + h * PACK, PACK)
                live = lax.broadcasted_iota(jnp.int32, (PACK, LANES), 0) + h * PACK < rank
                for v in range(nv):
                    pieces = [acc[g, pl.ds(first, PACK), v * size : (v + 1) * size] for g in range(ways)]
                    coef = jnp.where(live, jnp.concatenate(pieces, axis=1), 0.0)
                    out_ref[i, h, v * PACK : (v + 1) * PACK, :LANES] = coef.astype(jnp.bfloat16)
                    other = (v + sources) % nv
                    signed = -coef if v >= sources else coef
                    out_ref[i, h, other * PACK : (other + 1) * PACK, LANES:] = signed.astype(jnp.bfloat16)


def left_kernel(nv, u_ref, b_ref, out_ref, total):
    count, _, width, ranks, columns = u_ref.shape
    step = pl.program_id(0)
    lane = lax.broadcasted_iota(jnp.int32, (1, 8, nv * PACK), 2) % PACK
    lower = lane < 8
    keep = lane % 8 == lax.broadcasted_iota(jnp.int32, (1, 8, nv * PACK), 1)
    blank = jnp.zeros((width * PACK, LANES - columns), jnp.bfloat16)
    sums = []
    for i in range(count):
        kept = None
        for h in range(ranks // PACK):
            rows = []
            for c in range(2):
                rows.append(u_ref[i, c, :, h * PACK : (h + 1) * PACK].reshape(width * PACK, columns))
                rows.append(blank)
            grid = lax.dot_general(
                jnp.concatenate(rows, axis=1),
                b_ref[i, h],
                (((1,), (1,)), ((), ())),
                preferred_element_type=jnp.float32,
            ).reshape(width, 2, 8, nv * PACK)
            part = jnp.where(lower, grid[:, 0], grid[:, 1])
            kept = part if kept is None else kept + part
        sums.append(jnp.sum(jnp.where(keep, kept, 0.0), axis=1))
    rows = count * width
    total[pl.ds(pl.multiple_of(step * rows, 8), rows), :] = jnp.concatenate(sums, axis=0).astype(total.dtype)

    @pl.when(step == pl.num_programs(0) - 1)
    def _():
        lanes = lax.broadcasted_iota(jnp.int32, (nv, nv * PACK), 1)
        part = lax.broadcasted_iota(jnp.int32, (nv, nv * PACK), 0)
        pick = (lanes // PACK == part).astype(jnp.float32)
        out_ref[...] = lax.dot_general(
            pick,
            total[...],
            (((1,), (1,)), ((), ())),
            precision=lax.Precision.HIGHEST,
            preferred_element_type=jnp.float32,
        ).astype(jnp.bfloat16)


def tile_product(v_bases, u_bases, ranks, x):
    count, _, width, depth, columns = v_bases.shape
    n_group, nv, _ = x.shape
    sources = nv // 2
    per_group = -(-columns // n_group)
    halves = depth // PACK
    ways = WAYS
    size = LANES // ways
    block = max(k for k in range(ways, 11, ways) if width % k == 0)
    rank_rows = jnp.pad(ranks, ((0, 0), (0, LANES - columns)))[:, None, :]
    coefs = pl.pallas_call(
        functools.partial(right_kernel, (sources, n_group, per_group, width, ways)),
        grid=(width // block,),
        in_specs=[
            pl.BlockSpec(x.shape, lambda s: (0, 0, 0)),
            pl.BlockSpec(rank_rows.shape, lambda s: (0, 0, 0)),
            pl.BlockSpec((count, 2, block, depth, columns), lambda s: (0, 0, s, 0, 0)),
        ],
        out_specs=pl.BlockSpec((count, halves, nv * PACK, 2 * LANES), lambda s: (0, 0, 0, 0)),
        out_shape=jax.ShapeDtypeStruct((count, halves, nv * PACK, 2 * LANES), jnp.bfloat16),
        scratch_shapes=[
            pltpu.VMEM((LANES * nv, LANES), jnp.float32),
            pltpu.VMEM((nv, LANES, LANES), jnp.float32),
            pltpu.VMEM((ways, nv, width // ways, LANES), jnp.float32),
            pltpu.VMEM((ways, count * depth, block // ways * 2 * LANES), jnp.bfloat16),
            pltpu.VMEM((ways, nv * size, block // ways * 2 * LANES), jnp.bfloat16),
            pltpu.VMEM((ways, count * depth, nv * size), jnp.float32),
        ],
        compiler_params=pltpu.CompilerParams(vmem_limit_bytes=48 * 1024 * 1024),
        cost_estimate=pl.CostEstimate(
            flops=4 * v_bases.size * nv, bytes_accessed=2 * v_bases.size, transcendentals=0
        ),
    )(x, rank_rows, v_bases)
    group = step_of(count, 4, width)
    return pl.pallas_call(
        functools.partial(left_kernel, nv),
        grid=(count // group,),
        in_specs=[
            pl.BlockSpec((group, 2, width, depth, columns), lambda s: (s, 0, 0, 0, 0)),
            pl.BlockSpec((group, halves, nv * PACK, 2 * LANES), lambda s: (s, 0, 0, 0)),
        ],
        out_specs=pl.BlockSpec((nv, count * width), lambda s: (0, 0)),
        out_shape=jax.ShapeDtypeStruct((nv, count * width), jnp.bfloat16),
        scratch_shapes=[pltpu.VMEM((count * width, nv * PACK), jnp.float32)],
        compiler_params=pltpu.CompilerParams(vmem_limit_bytes=48 * 1024 * 1024),
        cost_estimate=pl.CostEstimate(
            flops=4 * u_bases.size * nv, bytes_accessed=2 * u_bases.size, transcendentals=0
        ),
    )(u_bases, coefs)


def angles_of(freq_bin, times, total):
    products = freq_bin[:, None] * times[None, :] % total
    return products.astype(jnp.float32) * (2.0 * math.pi / total)


def gather_all(piece, axis):
    count = lax.axis_size(axis)
    me = lax.axis_index(axis)
    pieces, owners = [piece], [me]
    for s in range(1, count):
        if count & (count - 1) == 0:
            perm = [(d, d ^ s) for d in range(count)]
            owners.append(me ^ s)
        else:
            perm = [(d, (d + s) % count) for d in range(count)]
            owners.append((me - s) % count)
        pieces.append(lax.ppermute(piece, axis, perm))
    return jnp.stack(pieces), jnp.stack(owners)


def local(virtual_source_trace, v_bases, u_bases, ranks, freq_bin, slab_order):
    n_tile = lax.axis_size("tile")
    n_freq = lax.axis_size("freq")
    devices = n_freq * n_tile
    steps_dev, sources, _ = virtual_source_trace.shape
    total = steps_dev * devices
    columns = v_bases.shape[2]
    width = v_bases.shape[5]
    rows_dev = v_bases.shape[1] * width
    both = ("freq", "tile")

    n_group = devices // sources
    per_group = -(-columns // n_group)
    lanes = round_up(per_group * width, LANES)
    raw = virtual_source_trace.reshape(steps_dev, sources, columns * width)
    raw = jnp.pad(raw, ((0, 0), (0, 0), (0, (n_group * per_group - columns) * width)))
    raw = raw.reshape(steps_dev, sources, n_group, per_group * width)
    raw = jnp.pad(raw, ((0, 0), (0, 0), (0, 0), (0, lanes - per_group * width)))
    raw = raw.transpose(1, 2, 0, 3).reshape(devices, steps_dev, lanes)
    raw = lax.all_to_all(raw, both, 0, 0, tiled=True).reshape(total, lanes)

    times = (slab_order[:, None] * steps_dev + jnp.arange(steps_dev, dtype=jnp.int32)[None, :]).reshape(total)
    angles = angles_of(freq_bin, times, total)
    forward = jnp.stack([jnp.cos(angles), -jnp.sin(angles)], axis=1) / math.sqrt(total)
    spectra = jnp.einsum("fct,tl->fcl", forward, raw.astype(jnp.float32), precision=lax.Precision.HIGHEST)
    spectra = spectra.astype(jnp.bfloat16)
    spectra = jnp.broadcast_to(spectra[:, None], (n_freq, n_tile, 2, lanes)).reshape(devices, 2, lanes)
    spectra = lax.all_to_all(spectra, both, 0, 0, tiled=True)
    spectra = spectra.reshape(sources, n_group, 2, lanes).transpose(1, 2, 0, 3)
    spectra = spectra.reshape(n_group, 2 * sources, lanes).astype(jnp.float32)

    order = (0, 2, 4, 3, 1)
    received = tile_product(v_bases[0].transpose(order), u_bases[0].transpose(order), ranks[0], spectra)

    gathered, owners = gather_all(received, "freq")
    gathered = gathered.reshape(n_freq, 2, sources, rows_dev).astype(jnp.float32)
    group = lax.dynamic_slice_in_dim(slab_order, lax.axis_index("freq") * n_tile, n_tile)
    times = (group[:, None] * steps_dev + jnp.arange(steps_dev, dtype=jnp.int32)[None, :]).reshape(-1)
    angles = angles_of(freq_bin[owners], times, total).T
    inverse = jnp.stack([jnp.cos(angles), -jnp.sin(angles)], axis=2) / math.sqrt(freq_bin.shape[0])
    wave = jnp.einsum("tgc,gcvn->tvn", inverse, gathered, precision=lax.Precision.HIGHEST)
    wave = wave.astype(jnp.bfloat16).reshape(n_tile, steps_dev, sources, rows_dev)
    wave = lax.all_to_all(wave, "tile", 0, 0, tiled=True)
    return wave.transpose(1, 2, 0, 3).reshape(steps_dev, sources, n_tile * rows_dev)


def solution(mesh):
    in_specs = (
        P(("freq", "tile"), None, None),
        P("freq", "tile", None, None, None, None),
        P("freq", "tile", None, None, None, None),
        P("freq", "tile", None),
        P(),
        P(),
    )
    out_specs = P(("freq", "tile"), None, None)
    return jax.shard_map(local, mesh=mesh, in_specs=in_specs, out_specs=out_specs, check_vma=False)
```
